512 devices in a mesh: pair: 128 (over z, y, core), blk: 4 (over x).
Axes of the slice: x: 4, y: 8, z: 8, core: 2. Of those that a mesh axis runs over, the one named last changes fastest.
Arguments:
- amplitudes: float32 [512, 16384], P('pair', 'blk'), may hold values from -6 to 6
- virt_ints: float32 [16384, 16384], P('blk', 'pair'), may hold values from -0.09375 to 0.09375
- virt_mask: int32 [128, 128], replicated, may hold values from 0 to 1, as said below
- hole_ints: float32 [512, 512], P('blk'), may hold values from -0.5 to 0.5
- hole_mask: int32 [4, 4], replicated, may hold values from 0 to 1, as said below
Outputs:
- residual: float32 [512, 16384], P('blk', 'pair')
The draws below stay inside these ranges and needn't reach their ends.
Inputs may be any that keep to these rules, and one draw needn't show every extreme that they name: `virt_mask`: split the 128 block rows into four equal groups in order; in every block column, each group holds exactly 8 ones. `hole_mask`: every block column holds exactly one 1.
All inputs are finite; a program needn't handle non-finite values.
Results may differ from the reference program's by a relative error of at most 0.000057.
Values sent between devices are 32-bit elements; how exact they have to be, the bound alone decides.
No kernel may reach another device: no remote copies, remote signals or barrier semaphores. Data moves between devices by JAX's collectives and lax.ppermute only.
A program may use at most 64 MiB of HBM per device.

```python
import jax
import jax.numpy as jnp
from jax import lax

NV = 16384
NO = 512
BS = 128


def draw_virt_mask(key, part):
    total_blocks = NV // BS
    group_blocks = total_blocks // 4
    per_group = group_blocks // 16 * 4
    scores = jax.random.randint(key, (4, total_blocks, group_blocks), 0, 1 << 20)
    scores = scores * group_blocks + jnp.arange(group_blocks, dtype=jnp.int32)[None, None, :]
    order = jnp.argsort(scores, axis=-1)
    ranks = jnp.argsort(order, axis=-1)
    chosen = (ranks < per_group).astype(jnp.int32)
    chosen = jnp.transpose(chosen, (0, 2, 1))
    return chosen.reshape(total_blocks, total_blocks)


def draw_hole_mask(key, part):
    total_blocks = NO // BS
    picked = jax.random.randint(key, (total_blocks,), 0, total_blocks)
    rows_ids = jnp.arange(total_blocks, dtype=jnp.int32)
    return (rows_ids[:, None] == picked[None, :]).astype(jnp.int32)


def steps_of(own_key, extent, cuts, smallest, high):
    def one(dim, parts):
        heights = jax.random.uniform(jax.random.fold_in(jax.random.fold_in(own_key, 6), dim), (parts,), jnp.float32, smallest / len(cuts), high / len(cuts))
        return jnp.repeat(jnp.exp(heights), extent[dim] // parts).reshape((-1,) + (1,) * (len(extent) - dim - 1))

    factor_of = one(*cuts[0])
    for cut in cuts[1:]:
        factor_of = factor_of * one(*cut)
    return factor_of


def normal_values(stream_key, dims, spread, bound, split=(), kind=jnp.bfloat16):
    values = spread * jax.random.normal(stream_key, dims, jnp.float32)
    if split:
        values = values * steps_of(stream_key, dims, split, -0.22, 0.18)
    return jnp.clip(values, -bound, bound).astype(kind)


def setup_inputs(seed: int = 0) -> dict:
    keys = jax.random.split(jax.random.key(seed), 6)
    return {
        "amplitudes": normal_values(keys[0], (NO, NV), 1.0, 6.0, ((0, 128), (1, 4)), jnp.float32),
        "virt_ints": normal_values(keys[1], (NV, NV), (NV // 4) ** -0.5, 0.09375, ((0, 4), (1, 128)), jnp.float32),
        "virt_mask": draw_virt_mask(jax.random.fold_in(keys[5], 71), 0),
        "hole_ints": normal_values(keys[3], (NO, NO), BS ** -0.5, 0.5, ((0, 4),), jnp.float32),
        "hole_mask": draw_hole_mask(jax.random.fold_in(keys[5], 71), 0),
    }


def expand_mask(mask, block):
    return jnp.repeat(jnp.repeat(mask, block, axis=0), block, axis=1).astype(jnp.float32)


def reference(amplitudes, virt_ints, virt_mask, hole_ints, hole_mask):
    virt_eff = virt_ints * expand_mask(virt_mask, BS)
    hole_eff = hole_ints * expand_mask(hole_mask, BS)
    particle = jnp.dot(amplitudes, virt_eff, precision=lax.Precision.HIGHEST)
    ladder = jnp.dot(hole_eff, amplitudes, precision=lax.Precision.HIGHEST)
    return particle + ladder
```

```python
import jax
import jax.numpy as jnp
from jax import lax
from jax.experimental import pallas as pl
from jax.experimental.pallas import tpu as pltpu
from jax.sharding import Mesh
from jax.sharding import PartitionSpec as P

BS = 128
PRECISE = lax.Precision.HIGHEST
PLANE = ("z", "y", "c")
SLOTS = 8


def pair_of(z, y, c):
    return z * 16 + y * 2 + c


FIRST = [[pair_of(z, y, 0) for z in range(8)] for y in range(8)] + [
    [pair_of(z, y, 1) for y in range(8)] for z in range(8)
]
SECOND = [[pair_of(z, y, 0) for y in range(8)] for z in range(8)] + [
    [pair_of(z, y, 1) for z in range(8)] for y in range(8)
]


def halves(low, high):
    rows = lax.broadcasted_iota(jnp.int32, (8, BS), 0)
    return jnp.where(rows < 4, low, high)


def swap(tile):
    return pltpu.roll(tile, 4, 0)


def pack_kernel(pos, slots, held, out, turned):
    c, z, y = pos[0], pos[1], pos[2]
    dest = pl.program_id(0)

    @pl.when(dest == 0)
    def _():
        def turn(two, _):
            for t in range(4):
                a, b = held[2 * t, two], held[2 * t + 1, two]
                turned[2 * two, t] = halves(a, swap(b))
                turned[2 * two + 1, t] = halves(swap(a), b)
            return 0

        lax.fori_loop(0, 16, turn, 0)

    own = jnp.where(c == 0, z * 16 + dest * 2, dest * 16 + y * 2 + 1)
    other = own + 1 - 2 * c
    for s in range(SLOTS):
        out[0, s] = turned[slots[s, own]]
        out[0, SLOTS + s] = turned[slots[s, other]]
    out[0, 2 * SLOTS] = turned[own % 32]
    out[0, 2 * SLOTS + 1] = turned[other % 32]


def pack(pos, slots, held):
    count = 2 * SLOTS + 2
    return pl.pallas_call(
        pack_kernel,
        grid_spec=pltpu.PrefetchScalarGridSpec(
            num_scalar_prefetch=2,
            grid=(8,),
            in_specs=[pl.BlockSpec((8, 16, 8, BS), lambda d, *_: (0, 0, 0, 0))],
            out_specs=pl.BlockSpec((1, count, 4, 8, BS), lambda d, *_: (d, 0, 0, 0, 0)),
            scratch_shapes=[pltpu.VMEM((32, 4, 8, BS), jnp.float32)],
        ),
        out_shape=jax.ShapeDtypeStruct((8, count, 4, 8, BS), jnp.float32),
        name="pack",
    )(pos, slots, held)


def take_kernel(pos, slots, block, out):
    out[0] = block[...]


def take_blocks(pos, slots, virt_ints):
    return pl.pallas_call(
        take_kernel,
        grid_spec=pltpu.PrefetchScalarGridSpec(
            num_scalar_prefetch=2,
            grid=(SLOTS,),
            in_specs=[pl.BlockSpec((BS, BS), lambda s, pos, slots: (slots[s, pos[4]], 0))],
            out_specs=pl.BlockSpec((1, BS, BS), lambda s, *_: (s, 0, 0)),
        ),
        out_shape=jax.ShapeDtypeStruct((SLOTS, BS, BS), jnp.float32),
        name="take",
    )(pos, slots, virt_ints)


def terms_kernel(pos, got, own, other, hole, out, ladder):
    c, z, x = pos[0], pos[1], pos[3]
    active = x == z // 2

    @pl.when(active)
    def _():
        owned = jnp.concatenate(
            [got[:, 2 * SLOTS].reshape(256, BS), got[:, 2 * SLOTS + 1].reshape(256, BS)], axis=1
        )
        for i in range(4):
            ladder[i] = jnp.dot(
                hole[i], owned, precision=PRECISE, preferred_element_type=jnp.float32
            )

    @pl.when(jnp.logical_not(active))
    def _():
        ladder[...] = jnp.zeros_like(ladder)

    for side, blocks in enumerate((own, other)):
        total = jnp.zeros((256, BS), jnp.float32)
        for s in range(0, SLOTS, 2):
            rows = jnp.concatenate(
                [
                    got[:, side * SLOTS + s].reshape(256, BS),
                    got[:, side * SLOTS + s + 1].reshape(256, BS),
                ],
                axis=1,
            )
            total += jnp.dot(
                rows,
                blocks[pl.ds(s, 2)].reshape(2 * BS, BS),
                precision=PRECISE,
                preferred_element_type=jnp.float32,
            )
        total = total.reshape(8, 4, 8, BS)
        first = jnp.where(side == 0, c, 1 - c) * 4
        none = jnp.zeros((8, BS), jnp.float32)

        def put(low, y, tile, i):
            at = pl.ds((low * 8 + y) * 8, 8)
            out[first + i, at] = tile + ladder[i, at, side * BS : (side + 1) * BS]

        @pl.when(c == 0)
        def _():
            for i in range(4):
                for y in range(8):
                    tile = total[y, i]
                    put(0, y, halves(tile, none), i)
                    put(1, y, halves(swap(tile), none), i)

        @pl.when(c == 1)
        def _():
            for i in range(4):
                for low in range(2):
                    for y in range(8):
                        tile = total[2 * i + low, y // 2]
                        put(low, y, halves(none, tile if y % 2 else swap(tile)), i)


def terms(pos, got, own, other, hole):
    whole = lambda shape: pl.BlockSpec(shape, lambda i, *_: (0,) * len(shape))
    args = (got, own, other, hole)
    return pl.pallas_call(
        terms_kernel,
        grid_spec=pltpu.PrefetchScalarGridSpec(
            num_scalar_prefetch=1,
            grid=(1,),
            in_specs=[whole(a.shape) for a in args],
            out_specs=whole((8, BS, BS)),
            scratch_shapes=[pltpu.VMEM((4, BS, 2 * BS), jnp.float32)],
        ),
        out_shape=jax.ShapeDtypeStruct((8, BS, BS), jnp.float32),
        compiler_params=pltpu.CompilerParams(vmem_limit_bytes=40 * 1024 * 1024),
        name="terms",
    )(pos, *args)


def slots_of(mask, x):
    slab = lax.dynamic_slice(mask, (x * 32, 0), (32, BS))
    ids = jnp.arange(32, dtype=jnp.int32)
    upto = (ids[:, None] >= ids[None, :]).astype(jnp.float32)
    rank = jnp.dot(upto, slab.astype(jnp.float32)).astype(jnp.int32)
    want = jnp.arange(1, SLOTS + 1, dtype=jnp.int32)
    hit = (rank[None] == want[:, None, None]) & (slab[None] == 1)
    return jnp.sum(jnp.where(hit, ids[None, :, None], 0), axis=1, dtype=jnp.int32)


def per_device(amplitudes, virt_ints, virt_mask, hole_ints, hole_mask):
    x, z, y, c = (lax.axis_index(a) for a in ("x", "z", "y", "c"))
    pos = jnp.stack([c, z, y, x, pair_of(z, y, c)]).astype(jnp.int32)
    slots = slots_of(virt_mask, x)

    blocks = amplitudes.reshape(4, 32, BS).transpose(1, 0, 2).reshape(1, 16, 8, BS)
    held = lax.all_to_all(
        jnp.broadcast_to(blocks, (8, 16, 8, BS)), PLANE, 0, 0, tiled=True, axis_index_groups=FIRST
    )

    own = take_blocks(pos, slots, virt_ints)
    other = lax.ppermute(own, "c", [(0, 1), (1, 0)])

    keep = jnp.repeat(lax.dynamic_slice(hole_mask, (x, 0), (1, 4)), BS, axis=1).astype(jnp.float32)
    col = jnp.arange(256, dtype=jnp.int32)
    second, first, r = col // 32, col // 4 % 8, col % 4
    wanted = jnp.where(c == 0, first * 64 + second * 8, second * 64 + first * 8 + 4) + r
    pick = (jnp.arange(512, dtype=jnp.int32)[:, None] == wanted[None, :]).astype(jnp.float32)
    hole_rows = jnp.dot(hole_ints * keep, pick, precision=PRECISE)
    hole = lax.all_gather(hole_rows, "x")

    sent = pack(pos, slots, held).reshape(8, 2 * SLOTS + 2, 32, BS)
    got = lax.all_to_all(sent, PLANE, 0, 0, tiled=True, axis_index_groups=SECOND)
    parts = terms(pos, got, own, other, hole)
    parts = lax.all_to_all(parts, ("c", "x"), 0, 0, tiled=True)
    return jnp.sum(parts, axis=0)


def solution(mesh):
    fine = Mesh(mesh.devices.reshape(8, 8, 2, 4), ("z", "y", "c", "x"))
    placed = (P(PLANE, "x"), P("x", PLANE), P(), P("x", None), P())
    return jax.shard_map(
        per_device, mesh=fine, in_specs=placed, out_specs=P("x", PLANE), check_vma=False
    )
```

```python
import jax
import jax.numpy as jnp
from jax import lax
from jax.experimental import pallas as pl
from jax.experimental.pallas import tpu as pltpu
from jax.sharding import Mesh
from jax.sharding import PartitionSpec as P

BS = 128
PLANE = ("z", "y", "c")
SLOTS = 8
MIB = 1024 * 1024
VMEM = pl.BlockSpec(memory_space=pltpu.VMEM)
SMEM = pl.BlockSpec(memory_space=pltpu.SMEM)


def pair_of(z, y, c):
    return z * 16 + y * 2 + c


FIRST = [[pair_of(z, y, 0) for z in range(8)] for y in range(8)] + [
    [pair_of(z, y, 1) for y in range(8)] for z in range(8)
]
SECOND = [[pair_of(z, y, 0) for y in range(8)] for z in range(8)] + [
    [pair_of(z, y, 1) for z in range(8)] for y in range(8)
]


def places():
    return tuple(lax.axis_index(a) for a in ("x", "z", "y", "c"))


def call(kernel, args, out, name, in_specs=None, scratch=(), limit=16):
    return pl.pallas_call(
        kernel,
        in_specs=in_specs or [VMEM] * len(args),
        out_specs=VMEM,
        out_shape=jax.ShapeDtypeStruct(out, jnp.float32),
        scratch_shapes=list(scratch),
        compiler_params=pltpu.CompilerParams(vmem_limit_bytes=limit * MIB),
        name=name,
    )(*args)


def halves(low, high):
    rows = lax.broadcasted_iota(jnp.int32, (8, BS), 0)
    return jnp.where(rows < 4, low, high)


def swap(tile):
    return pltpu.roll(tile, 4, 0)


def pack_kernel(slots, held, out, turned):
    x, z, y, c = places()
    dest = pl.program_id(0)

    @pl.when(dest == 0)
    def _():
        for b in range(32):
            at = slice(b * BS, (b + 1) * BS)
            for t in range(4):
                for h in range(2):
                    turned[b, t, 4 * h : 4 * h + 4] = held[2 * t + h, :, at]

    own = jnp.where(c == 0, z * 16 + dest * 2, dest * 16 + y * 2 + 1)
    other = own + 1 - 2 * c
    for side, column in enumerate((own, other)):
        for s in range(SLOTS):
            out[0, side * SLOTS + s] = turned[slots[s, column]]
        out[0, 2 * SLOTS + side] = turned[column % 32]


def pack(slots, held):
    count = 2 * SLOTS + 2
    return pl.pallas_call(
        pack_kernel,
        grid=(8,),
        in_specs=[SMEM, VMEM],
        out_specs=pl.BlockSpec((1, count, 4, 8, BS), lambda d: (d, 0, 0, 0, 0)),
        out_shape=jax.ShapeDtypeStruct((8, count, 4, 8, BS), jnp.float32),
        scratch_shapes=[pltpu.VMEM((32, 4, 8, BS), jnp.float32)],
        compiler_params=pltpu.CompilerParams(vmem_limit_bytes=16 * MIB),
        name="pack",
    )(slots, held)


def take_kernel(slots, ints, out, sems):
    x, z, y, c = places()
    mine = pair_of(z, y, c)
    copies = []
    for s in range(SLOTS):
        rows = pl.ds(pl.multiple_of(slots[s, mine] * BS, BS), BS)
        copies.append(pltpu.make_async_copy(ints.at[rows], out.at[s], sems.at[s]))
        copies[-1].start()
    for copy in copies:
        copy.wait()


def take(slots, ints):
    return call(
        take_kernel,
        (slots, ints),
        (SLOTS, BS, BS),
        "take",
        in_specs=[SMEM, pl.BlockSpec(memory_space=pl.ANY)],
        scratch=[pltpu.SemaphoreType.DMA((SLOTS,))],
        limit=4,
    )


def parted(value):
    high = value.astype(jnp.bfloat16)
    return high, (value - high.astype(jnp.float32)).astype(jnp.bfloat16)


def product(left, right):
    dot = lambda a, b: jnp.dot(a, b, preferred_element_type=jnp.float32)
    (a, b), (p, q) = parted(left), parted(right)
    return dot(a, p) + (dot(a, q) + dot(b, p))


def terms_kernel(got, own, other, hole, out):
    x, z, y, c = places()
    active = x == z // 2
    firsts = (c * 4, 4 - c * 4)
    column = lambda at: got[:, at].reshape(256, BS)

    @pl.when(active)
    def _():
        owned = jnp.concatenate([column(2 * SLOTS), column(2 * SLOTS + 1)], axis=1)
        for i in range(4):
            ladder = product(hole[i], owned)
            for side in range(2):
                out[firsts[side] + i] = ladder[:, side * BS : (side + 1) * BS]

    @pl.when(jnp.logical_not(active))
    def _():
        out[...] = jnp.zeros_like(out)

    for side, blocks in enumerate((own, other)):
        total = jnp.zeros((256, BS), jnp.float32)
        for s in range(0, SLOTS, 2):
            at = side * SLOTS + s
            rows = jnp.concatenate([column(at), column(at + 1)], axis=1)
            total += product(rows, blocks[s : s + 2].reshape(2 * BS, BS))
        total = total.reshape(8, 4, 8, BS)
        none = jnp.zeros((8, BS), jnp.float32)

        def put(i, low, row, tile, side=side):
            at = slice((low * 8 + row) * 8, (low * 8 + row) * 8 + 8)
            out[firsts[side] + i, at] += tile

        @pl.when(c == 0)
        def _():
            for i in range(4):
                for row in range(8):
                    tile = total[row, i]
                    put(i, 0, row, halves(tile, none))
                    put(i, 1, row, halves(swap(tile), none))

        @pl.when(c == 1)
        def _():
            for i in range(4):
                for low in range(2):
                    for row in range(8):
                        tile = total[2 * i + low, row // 2]
                        put(i, low, row, halves(none, tile if row % 2 else swap(tile)))


def slots_of(mask, x):
    slab = lax.dynamic_slice(mask, (x * 32, 0), (32, BS))
    ids = jnp.arange(32, dtype=jnp.int32)
    upto = (ids[:, None] >= ids[None, :]).astype(jnp.float32)
    rank = jnp.dot(upto, slab.astype(jnp.float32)).astype(jnp.int32)
    want = jnp.arange(1, SLOTS + 1, dtype=jnp.int32)
    hit = (rank[None] == want[:, None, None]) & (slab[None] == 1)
    return jnp.sum(jnp.where(hit, ids[None, :, None], 0), axis=1, dtype=jnp.int32)


def per_device(amplitudes, virt_ints, virt_mask, hole_ints, hole_mask):
    x, z, y, c = places()
    held = lax.all_to_all(
        jnp.broadcast_to(amplitudes[None], (8, 4, 32 * BS)),
        PLANE, 0, 0, tiled=True, axis_index_groups=FIRST,
    )
    slots = slots_of(virt_mask, x)
    own = take(slots, virt_ints)
    other = lax.ppermute(own, "c", [(0, 1), (1, 0)])
    held, own = lax.optimization_barrier((held, own))

    keep = jnp.repeat(lax.dynamic_slice(hole_mask, (x, 0), (1, 4)), BS, axis=1).astype(jnp.float32)
    col = jnp.arange(256, dtype=jnp.int32)
    second, first, r = col // 32, col // 4 % 8, col % 4
    wanted = jnp.where(c == 0, first * 64 + second * 8, second * 64 + first * 8 + 4) + r
    pick = (jnp.arange(512, dtype=jnp.int32)[:, None] == wanted[None, :]).astype(jnp.float32)
    hole_rows = jnp.dot(hole_ints * keep, pick, precision=lax.Precision.HIGHEST)
    hole = lax.all_gather(hole_rows, "x")

    got = lax.all_to_all(
        pack(slots, held), PLANE, 0, 0, tiled=True, axis_index_groups=SECOND
    )
    parts = call(terms_kernel, (got, own, other, hole), (8, BS, BS), "terms")
    parts = lax.all_to_all(parts, ("c", "x"), 0, 0, tiled=True)
    return jnp.sum(parts, axis=0)


def solution(mesh):
    fine = Mesh(mesh.devices.reshape(8, 8, 2, 4), ("z", "y", "c", "x"))
    placed = (P(PLANE, "x"), P("x", PLANE), P(), P("x", None), P())
    return jax.shard_map(
        per_device, mesh=fine, in_specs=placed, out_specs=P("x", PLANE), check_vma=False
    )
```

```python
import jax
import jax.numpy as jnp
from jax import lax
from jax.experimental import pallas as pl
from jax.experimental.pallas import tpu as pltpu
from jax.sharding import Mesh
from jax.sharding import PartitionSpec as P

BS = 128
PLANE = ("z", "y", "c")
SLOTS = 8
MIB = 1024 * 1024
VMEM = pl.BlockSpec(memory_space=pltpu.VMEM)
SMEM = pl.BlockSpec(memory_space=pltpu.SMEM)
HBM = pl.BlockSpec(memory_space=pltpu.HBM)


def pair_of(z, y, c):
    return z * 16 + y * 2 + c


FIRST = [[pair_of(z, y, 0) for z in range(8)] for y in range(8)] + [
    [pair_of(z, y, 1) for y in range(8)] for z in range(8)
]
SECOND = [[pair_of(z, y, 0) for y in range(8)] for z in range(8)] + [
    [pair_of(z, y, 1) for z in range(8)] for y in range(8)
]


def places():
    return tuple(lax.axis_index(a) for a in ("x", "z", "y", "c"))


def call(kernel, args, out, name, in_specs=None, out_specs=VMEM, scratch=(), limit=16):
    return pl.pallas_call(
        kernel,
        in_specs=in_specs or [VMEM] * len(args),
        out_specs=out_specs,
        out_shape=jax.ShapeDtypeStruct(out, jnp.float32),
        scratch_shapes=list(scratch),
        compiler_params=pltpu.CompilerParams(vmem_limit_bytes=limit * MIB),
        name=name,
    )(*args)


def halves(low, high):
    rows = lax.broadcasted_iota(jnp.int32, (8, BS), 0)
    return jnp.where(rows < 4, low, high)


def swap(tile):
    return pltpu.roll(tile, 4, 0)


def spread_kernel(held, out, sems):
    copies = [pltpu.make_async_copy(held, out.at[k], sems.at[k]) for k in range(8)]
    for copy in copies:
        copy.start()
    for copy in copies:
        copy.wait()


def spread(held):
    return call(
        spread_kernel,
        (held,),
        (8,) + held.shape,
        "spread",
        in_specs=[HBM],
        out_specs=HBM,
        scratch=[pltpu.SemaphoreType.DMA((8,))],
        limit=60,
    )


def pack_kernel(slots, held, out, turned, ready, sems):
    x, z, y, c = places()
    for b in range(32):
        at = slice(b * BS, (b + 1) * BS)
        for t in range(4):
            for h in range(2):
                turned[b, t, 4 * h : 4 * h + 4] = held[2 * t + h, :, at]

    def copy(dest):
        return pltpu.make_async_copy(ready.at[dest], out.at[dest], sems.at[dest])

    def send(dest, _):
        own = jnp.where(c == 0, z * 16 + dest * 2, dest * 16 + y * 2 + 1)
        other = own + 1 - 2 * c
        for side, column in enumerate((own, other)):
            for s in range(SLOTS):
                ready[dest, side * SLOTS + s] = turned[slots[s, column]]
            ready[dest, 2 * SLOTS + side] = turned[column % 32]
        copy(dest).start()
        return 0

    lax.fori_loop(0, 8, send, 0)
    for dest in range(8):
        copy(dest).wait()


def pack(slots, held):
    shape = (8, 2 * SLOTS + 2, 4, 8, BS)
    return call(
        pack_kernel,
        (slots, held),
        shape,
        "pack",
        in_specs=[SMEM, VMEM],
        out_specs=HBM,
        scratch=[
            pltpu.VMEM((32, 4, 8, BS), jnp.float32),
            pltpu.VMEM(shape, jnp.float32),
            pltpu.SemaphoreType.DMA((8,)),
        ],
        limit=58,
    )


def take_kernel(slots, ints, out, sems):
    x, z, y, c = places()
    mine = pair_of(z, y, c)
    copies = []
    for s in range(SLOTS):
        rows = pl.ds(pl.multiple_of(slots[s, mine] * BS, BS), BS)
        copies.append(pltpu.make_async_copy(ints.at[rows], out.at[s], sems.at[s]))
        copies[-1].start()
    for copy in copies:
        copy.wait()


def take(slots, ints):
    return call(
        take_kernel,
        (slots, ints),
        (SLOTS, BS, BS),
        "take",
        in_specs=[SMEM, HBM],
        scratch=[pltpu.SemaphoreType.DMA((SLOTS,))],
        limit=59,
    )


def parted(value):
    high = value.astype(jnp.bfloat16)
    return high, (value - high.astype(jnp.float32)).astype(jnp.bfloat16)


def product(left, right):
    dot = lambda a, b: jnp.dot(a, b, preferred_element_type=jnp.float32)
    (a, b), (p, q) = parted(left), parted(right)
    return dot(a, p) + (dot(a, q) + dot(b, p))


def terms_kernel(side, got, blocks, hole, out):
    x, z, y, c = places()
    active = x == z // 2
    column = lambda at: got[:, at].reshape(256, BS)

    @pl.when(active)
    def _():
        ladder = product(hole[...].reshape(4 * BS, 2 * BS), column(2 * SLOTS + side))
        out[...] = ladder.reshape(4, BS, BS)

    @pl.when(jnp.logical_not(active))
    def _():
        out[...] = jnp.zeros_like(out)

    total = jnp.zeros((256, BS), jnp.float32)
    for s in range(0, SLOTS, 2):
        at = side * SLOTS + s
        rows = jnp.concatenate([column(at), column(at + 1)], axis=1)
        total += product(rows, blocks[s : s + 2].reshape(2 * BS, BS))
    total = total.reshape(8, 4, 8, BS)
    none = jnp.zeros((8, BS), jnp.float32)

    def put(i, low, row, tile):
        at = slice((low * 8 + row) * 8, (low * 8 + row) * 8 + 8)
        out[i, at] += tile

    @pl.when(c == 0)
    def _():
        for i in range(4):
            for row in range(8):
                tile = total[row, i]
                put(i, 0, row, halves(tile, none))
                put(i, 1, row, halves(swap(tile), none))

    @pl.when(c == 1)
    def _():
        for i in range(4):
            for low in range(2):
                for row in range(8):
                    tile = total[2 * i + low, row // 2]
                    put(i, low, row, halves(none, tile if row % 2 else swap(tile)))


def terms(side, got, blocks, hole):
    return call(
        lambda *refs: terms_kernel(side, *refs),
        (got, blocks, hole),
        (4, BS, BS),
        "other_terms" if side else "own_terms",
    )


def slots_of(mask, x):
    slab = lax.dynamic_slice(mask, (x * 32, 0), (32, BS))
    ids = jnp.arange(32, dtype=jnp.int32)
    upto = (ids[:, None] >= ids[None, :]).astype(jnp.float32)
    rank = jnp.dot(upto, slab.astype(jnp.float32)).astype(jnp.int32)
    want = jnp.arange(1, SLOTS + 1, dtype=jnp.int32)
    hit = (rank[None] == want[:, None, None]) & (slab[None] == 1)
    return jnp.sum(jnp.where(hit, ids[None, :, None], 0), axis=1, dtype=jnp.int32)


def per_device(amplitudes, virt_ints, virt_mask, hole_ints, hole_mask):
    x, z, y, c = places()
    held = lax.all_to_all(
        spread(amplitudes),
        PLANE, 0, 0, tiled=True, axis_index_groups=FIRST,
    )
    slots = slots_of(virt_mask, x)
    own = take(slots, virt_ints)
    other = lax.ppermute(own, "c", [(0, 1), (1, 0)])
    held, own = lax.optimization_barrier((held, own))

    keep = jnp.repeat(lax.dynamic_slice(hole_mask, (x, 0), (1, 4)), BS, axis=1).astype(jnp.float32)
    col = jnp.arange(256, dtype=jnp.int32)
    second, first, r = col // 32, col // 4 % 8, col % 4
    wanted = jnp.where(c == 0, first * 64 + second * 8, second * 64 + first * 8 + 4) + r
    pick = (jnp.arange(512, dtype=jnp.int32)[:, None] == wanted[None, :]).astype(jnp.float32)
    hole_rows = jnp.dot(hole_ints * keep, pick, precision=lax.Precision.HIGHEST)
    hole = lax.all_gather(hole_rows, "x")

    got = lax.all_to_all(
        pack(slots, held), PLANE, 0, 0, tiled=True, axis_index_groups=SECOND
    )
    theirs = terms(1, got, other, hole)
    mine = terms(0, got, own, hole)
    parts = mine + lax.ppermute(theirs, "c", [(0, 1), (1, 0)])
    return jnp.sum(lax.all_to_all(parts, "x", 0, 0, tiled=True), axis=0)


def solution(mesh):
    fine = Mesh(mesh.devices.reshape(8, 8, 2, 4), ("z", "y", "c", "x"))
    placed = (P(PLANE, "x"), P("x", PLANE), P(), P("x", None), P())
    return jax.shard_map(
        per_device, mesh=fine, in_specs=placed, out_specs=P("x", PLANE), check_vma=False
    )
```

```python
import jax
import jax.numpy as jnp
from jax import lax
from jax.experimental import pallas as pl
from jax.experimental.pallas import tpu as pltpu
from jax.sharding import Mesh
from jax.sharding import PartitionSpec as P

BS = 128
PLANE = ("z", "y", "c")
SLOTS = 8
MIB = 1024 * 1024
VMEM = pl.BlockSpec(memory_space=pltpu.VMEM)
SMEM = pl.BlockSpec(memory_space=pltpu.SMEM)
HBM = pl.BlockSpec(memory_space=pltpu.HBM)


def pair_of(z, y, c):
    return z * 16 + y * 2 + c


FIRST = [[pair_of(z, y, 0) for z in range(8)] for y in range(8)] + [
    [pair_of(z, y, 1) for y in range(8)] for z in range(8)
]
SECOND = [[pair_of(z, y, 0) for y in range(8)] for z in range(8)] + [
    [pair_of(z, y, 1) for z in range(8)] for y in range(8)
]


def places():
    return tuple(lax.axis_index(a) for a in ("x", "z", "y", "c"))


def call(kernel, args, out, name, in_specs=None, out_specs=VMEM, scratch=(), limit=16):
    return pl.pallas_call(
        kernel,
        in_specs=in_specs or [VMEM] * len(args),
        out_specs=out_specs,
        out_shape=jax.ShapeDtypeStruct(out, jnp.float32),
        scratch_shapes=list(scratch),
        compiler_params=pltpu.CompilerParams(vmem_limit_bytes=limit * MIB),
        name=name,
    )(*args)


def halves(low, high):
    rows = lax.broadcasted_iota(jnp.int32, (8, BS), 0)
    return jnp.where(rows < 4, low, high)


def swap(tile):
    return pltpu.roll(tile, 4, 0)


def spread_kernel(held, out):
    for k in range(8):
        out[k] = held[...]


def spread(held):
    return call(spread_kernel, (held,), (8,) + held.shape, "spread", limit=60)


def pack_kernel(slots, held, out, turned, ready, sems):
    x, z, y, c = places()
    for b in range(32):
        at = slice(b * BS, (b + 1) * BS)
        for t in range(4):
            for h in range(2):
                turned[b, t, 4 * h : 4 * h + 4] = held[2 * t + h, :, at]

    def copy(dest):
        return pltpu.make_async_copy(ready.at[dest], out.at[dest], sems.at[dest])

    def send(dest, _):
        own = jnp.where(c == 0, z * 16 + dest * 2, dest * 16 + y * 2 + 1)
        other = own + 1 - 2 * c
        for side, column in enumerate((own, other)):
            for s in range(SLOTS):
                ready[dest, side * SLOTS + s] = turned[slots[s, column]]
            ready[dest, 2 * SLOTS + side] = turned[column % 32]
        copy(dest).start()
        return 0

    lax.fori_loop(0, 8, send, 0)
    for dest in range(8):
        copy(dest).wait()


def pack(slots, held):
    shape = (8, 2 * SLOTS + 2, 4, 8, BS)
    return call(
        pack_kernel,
        (slots, held),
        shape,
        "pack",
        in_specs=[SMEM, VMEM],
        out_specs=HBM,
        scratch=[
            pltpu.VMEM((32, 4, 8, BS), jnp.float32),
            pltpu.VMEM(shape, jnp.float32),
            pltpu.SemaphoreType.DMA((8,)),
        ],
        limit=52,
    )


def take_kernel(slots, ints, out, sems):
    x, z, y, c = places()
    mine = pair_of(z, y, c)
    copies = []
    for s in range(SLOTS):
        rows = pl.ds(pl.multiple_of(slots[s, mine] * BS, BS), BS)
        copies.append(pltpu.make_async_copy(ints.at[rows], out.at[s], sems.at[s]))
        copies[-1].start()
    for copy in copies:
        copy.wait()


def take(slots, ints):
    return call(
        take_kernel,
        (slots, ints),
        (SLOTS, BS, BS),
        "take",
        in_specs=[SMEM, pl.BlockSpec(memory_space=pl.ANY)],
        scratch=[pltpu.SemaphoreType.DMA((SLOTS,))],
        limit=4,
    )


def parted(value):
    high = value.astype(jnp.bfloat16)
    return high, (value - high.astype(jnp.float32)).astype(jnp.bfloat16)


def product(left, right):
    dot = lambda a, b: jnp.dot(a, b, preferred_element_type=jnp.float32)
    (a, b), (p, q) = parted(left), parted(right)
    wide = dot(a, jnp.concatenate([p, q], axis=1))
    width = right.shape[1]
    return wide[:, :width] + (wide[:, width:] + dot(b, p))


def terms_kernel(got, own, far, hole, out, other, sem):
    x, z, y, c = places()
    copy = pltpu.make_async_copy(far, other, sem)
    copy.start()
    active = x == z // 2
    firsts = (c * 4, 4 - c * 4)
    column = lambda at: got[:, at].reshape(256, BS)

    @pl.when(active)
    def _():
        for side in range(2):
            ladder = product(hole[...].reshape(4 * BS, 2 * BS), column(2 * SLOTS + side))
            out[pl.ds(firsts[side], 4)] = ladder.reshape(4, BS, BS)

    @pl.when(jnp.logical_not(active))
    def _():
        out[...] = jnp.zeros_like(out)

    for side, blocks in enumerate((own, other)):
        if side:
            copy.wait()
        total = jnp.zeros((256, BS), jnp.float32)
        for s in range(0, SLOTS, 2):
            at = side * SLOTS + s
            rows = jnp.concatenate([column(at), column(at + 1)], axis=1)
            total += product(rows, blocks[s : s + 2].reshape(2 * BS, BS))
        total = total.reshape(8, 4, 8, BS)
        none = jnp.zeros((8, BS), jnp.float32)

        def put(i, low, row, tile, side=side):
            at = slice((low * 8 + row) * 8, (low * 8 + row) * 8 + 8)
            out[firsts[side] + i, at] += tile

        @pl.when(c == 0)
        def _():
            for i in range(4):
                for row in range(8):
                    tile = total[row, i]
                    put(i, 0, row, halves(tile, none))
                    put(i, 1, row, halves(swap(tile), none))

        @pl.when(c == 1)
        def _():
            for i in range(4):
                for low in range(2):
                    for row in range(8):
                        tile = total[2 * i + low, row // 2]
                        put(i, low, row, halves(none, tile if row % 2 else swap(tile)))


def slots_of(mask, x):
    slab = lax.dynamic_slice(mask, (x * 32, 0), (32, BS))
    ids = jnp.arange(32, dtype=jnp.int32)
    upto = (ids[:, None] >= ids[None, :]).astype(jnp.float32)
    rank = jnp.dot(upto, slab.astype(jnp.float32)).astype(jnp.int32)
    want = jnp.arange(1, SLOTS + 1, dtype=jnp.int32)
    hit = (rank[None] == want[:, None, None]) & (slab[None] == 1)
    return jnp.sum(jnp.where(hit, ids[None, :, None], 0), axis=1, dtype=jnp.int32)


def per_device(amplitudes, virt_ints, virt_mask, hole_ints, hole_mask):
    x, z, y, c = places()
    held = lax.all_to_all(
        spread(amplitudes),
        PLANE, 0, 0, tiled=True, axis_index_groups=FIRST,
    )
    slots = slots_of(virt_mask, x)
    own = take(slots, virt_ints)
    other = lax.ppermute(own, "c", [(0, 1), (1, 0)])
    held, own = lax.optimization_barrier((held, own))

    keep = jnp.repeat(lax.dynamic_slice(hole_mask, (x, 0), (1, 4)), BS, axis=1).astype(jnp.float32)
    col = jnp.arange(256, dtype=jnp.int32)
    second, first, r = col // 32, col // 4 % 8, col % 4
    wanted = jnp.where(c == 0, first * 64 + second * 8, second * 64 + first * 8 + 4) + r
    pick = (jnp.arange(512, dtype=jnp.int32)[:, None] == wanted[None, :]).astype(jnp.float32)
    hole_rows = jnp.dot(hole_ints * keep, pick, precision=lax.Precision.HIGHEST)
    hole = lax.all_gather(hole_rows, "x")

    got = lax.all_to_all(
        pack(slots, held), PLANE, 0, 0, tiled=True, axis_index_groups=SECOND
    )
    parts = call(
        terms_kernel,
        (got, own, other, hole),
        (8, BS, BS),
        "terms",
        in_specs=[VMEM, VMEM, pl.BlockSpec(memory_space=pl.ANY), VMEM],
        scratch=[pltpu.VMEM((SLOTS, BS, BS), jnp.float32), pltpu.SemaphoreType.DMA],
    )
    parts = lax.all_to_all(parts, ("c", "x"), 0, 0, tiled=True)
    return jnp.sum(parts, axis=0)


def solution(mesh):
    fine = Mesh(mesh.devices.reshape(8, 8, 2, 4), ("z", "y", "c", "x"))
    placed = (P(PLANE, "x"), P("x", PLANE), P(), P("x", None), P())
    return jax.shard_map(
        per_device, mesh=fine, in_specs=placed, out_specs=P("x", PLANE), check_vma=False
    )
```

```python
import jax
import jax.numpy as jnp
from jax import lax
from jax.experimental import pallas as pl
from jax.experimental.pallas import tpu as pltpu
from jax.sharding import Mesh
from jax.sharding import PartitionSpec as P

BS = 128
PLANE = ("z", "y", "c")
SLOTS = 8
MIB = 1024 * 1024
VMEM = pl.BlockSpec(memory_space=pltpu.VMEM)
SMEM = pl.BlockSpec(memory_space=pltpu.SMEM)
HBM = pl.BlockSpec(memory_space=pltpu.HBM)


def pair_of(z, y, c):
    return z * 16 + y * 2 + c


FIRST = [[pair_of(z, y, 0) for z in range(8)] for y in range(8)] + [
    [pair_of(z, y, 1) for y in range(8)] for z in range(8)
]
SECOND = [[pair_of(z, y, 0) for y in range(8)] for z in range(8)] + [
    [pair_of(z, y, 1) for z in range(8)] for y in range(8)
]


def places():
    return tuple(lax.axis_index(a) for a in ("x", "z", "y", "c"))


def call(kernel, args, out, name, in_specs=None, out_specs=VMEM, scratch=(), limit=16):
    return pl.pallas_call(
        kernel,
        in_specs=in_specs or [VMEM] * len(args),
        out_specs=out_specs,
        out_shape=jax.ShapeDtypeStruct(out, jnp.float32),
        scratch_shapes=list(scratch),
        compiler_params=pltpu.CompilerParams(vmem_limit_bytes=limit * MIB),
        name=name,
    )(*args)


def halves(low, high):
    rows = lax.broadcasted_iota(jnp.int32, (8, BS), 0)
    return jnp.where(rows < 4, low, high)


def swap(tile):
    return pltpu.roll(tile, 4, 0)


def spread_kernel(held, out):
    for k in range(8):
        out[k] = held[...]


def spread(held):
    return call(spread_kernel, (held,), (8,) + held.shape, "spread", limit=60)


def pack_kernel(slots, held, out, turned, ready, sems):
    x, z, y, c = places()
    for b in range(32):
        at = slice(b * BS, (b + 1) * BS)
        for t in range(4):
            for h in range(2):
                turned[b, t, 4 * h : 4 * h + 4] = held[2 * t + h, :, at]

    def copy(dest):
        return pltpu.make_async_copy(ready.at[dest], out.at[dest], sems.at[dest])

    def send(dest, _):
        own = jnp.where(c == 0, z * 16 + dest * 2, dest * 16 + y * 2 + 1)
        other = own + 1 - 2 * c
        for side, column in enumerate((own, other)):
            for s in range(SLOTS):
                ready[dest, side * SLOTS + s] = turned[slots[s, column]]
            ready[dest, 2 * SLOTS + side] = turned[column % 32]
        copy(dest).start()
        return 0

    lax.fori_loop(0, 8, send, 0)
    for dest in range(8):
        copy(dest).wait()


def pack(slots, held):
    shape = (8, 2 * SLOTS + 2, 4, 8, BS)
    return call(
        pack_kernel,
        (slots, held),
        shape,
        "pack",
        in_specs=[SMEM, VMEM],
        out_specs=HBM,
        scratch=[
            pltpu.VMEM((32, 4, 8, BS), jnp.float32),
            pltpu.VMEM(shape, jnp.float32),
            pltpu.SemaphoreType.DMA((8,)),
        ],
        limit=52,
    )


def take_kernel(slots, ints, out, sems):
    x, z, y, c = places()
    mine = pair_of(z, y, c)
    copies = []
    for s in range(SLOTS):
        rows = pl.ds(pl.multiple_of(slots[s, mine] * BS, BS), BS)
        copies.append(pltpu.make_async_copy(ints.at[rows], out.at[s], sems.at[s]))
        copies[-1].start()
    for copy in copies:
        copy.wait()


def take(slots, ints):
    return call(
        take_kernel,
        (slots, ints),
        (SLOTS, BS, BS),
        "take",
        in_specs=[SMEM, pl.BlockSpec(memory_space=pl.ANY)],
        scratch=[pltpu.SemaphoreType.DMA((SLOTS,))],
        limit=4,
    )


def parted(value):
    high = value.astype(jnp.bfloat16)
    return high, (value - high.astype(jnp.float32)).astype(jnp.bfloat16)


def product(left, right):
    dot = lambda a, b: jnp.dot(a, b, preferred_element_type=jnp.float32)
    (a, b), (p, q) = parted(left), parted(right)
    wide = dot(a, jnp.concatenate([p, q], axis=1))
    width = right.shape[1]
    return wide[:, :width] + (wide[:, width:] + dot(b, p))


def particle_kernel(got, own, far, out, other, sem):
    copy = pltpu.make_async_copy(far, other, sem)
    copy.start()
    column = lambda at: got[:, at].reshape(256, BS)
    for side, blocks in enumerate((own, other)):
        if side:
            copy.wait()
        total = jnp.zeros((256, BS), jnp.float32)
        for s in range(0, SLOTS, 2):
            at = side * SLOTS + s
            rows = jnp.concatenate([column(at), column(at + 1)], axis=1)
            total += product(rows, blocks[s : s + 2].reshape(2 * BS, BS))
        out[side] = total.reshape(8, 4, 8, BS)


def terms_kernel(total, got, swapped, hole, out):
    x, z, y, c = places()
    firsts = (c * 4, 4 - c * 4)
    for side in range(2):

        @pl.when(c == 0)
        def _():
            for i in range(4):
                out[firsts[side] + i] = total[side, :, i]

        @pl.when(c == 1)
        def _():
            for i in range(4):
                out[firsts[side] + i] = total[side, 2 * i : 2 * i + 2].reshape(8, 8, BS)

        @pl.when(x == z // 2)
        def _():
            rows = jnp.concatenate(
                [
                    got[:, 2 * SLOTS + side].reshape(256, BS),
                    swapped[:, 1 - side].reshape(256, BS),
                ],
                axis=0,
            )
            ladder = product(hole[...].reshape(256, 512), rows).reshape(4, 8, 8, BS)
            out[pl.ds(firsts[side], 4)] += ladder


def add_kernel(parts, out):
    a, b = (parts[k] + parts[k + 1] + parts[k + 2] + parts[k + 3] for k in (0, 4))
    for low in range(2):
        for row in range(8):
            u, v = a[row], b[low * 4 + row // 2]
            at = (low * 8 + row) * 8
            out[at : at + 8] = halves(swap(u) if low else u, v if row % 2 else swap(v))


def slots_of(mask, x):
    slab = lax.dynamic_slice(mask, (x * 32, 0), (32, BS))
    ids = jnp.arange(32, dtype=jnp.int32)
    upto = (ids[:, None] >= ids[None, :]).astype(jnp.float32)
    rank = jnp.dot(upto, slab.astype(jnp.float32)).astype(jnp.int32)
    want = jnp.arange(1, SLOTS + 1, dtype=jnp.int32)
    hit = (rank[None] == want[:, None, None]) & (slab[None] == 1)
    return jnp.sum(jnp.where(hit, ids[None, :, None], 0), axis=1, dtype=jnp.int32)


def per_device(amplitudes, virt_ints, virt_mask, hole_ints, hole_mask):
    x, z, y, c = places()
    held = lax.all_to_all(
        spread(amplitudes),
        PLANE, 0, 0, tiled=True, axis_index_groups=FIRST,
    )
    slots = slots_of(virt_mask, x)
    own = take(slots, virt_ints)
    other = lax.ppermute(own, "c", [(0, 1), (1, 0)])
    held, own = lax.optimization_barrier((held, own))

    keep = jnp.repeat(lax.dynamic_slice(hole_mask, (x, 0), (1, 4)), BS, axis=1).astype(jnp.float32)
    ids = jnp.arange(512, dtype=jnp.int32)
    second, first, r = ids % 256 // 32, ids // 4 % 8, ids % 4
    kind = jnp.where(ids < 256, c, 1 - c)
    wanted = jnp.where(kind == 0, first * 64 + second * 8, second * 64 + first * 8 + 4) + r
    columns = (ids[:, None] == wanted[None, :]).astype(jnp.float32)
    row = jnp.arange(64, dtype=jnp.int32)
    start = jnp.where(c == 0, row // 4 % 2 * 64 + row // 8 * 8, row // 4 * 8 + 4) + row % 4
    rows = (start[:, None] == ids[None, :BS]).astype(jnp.float32)
    exact = lambda a, b: jnp.dot(a, b, precision=lax.Precision.HIGHEST)
    hole = lax.all_gather(exact(exact(rows, hole_ints * keep), columns), "x")

    got = lax.all_to_all(
        pack(slots, held), PLANE, 0, 0, tiled=True, axis_index_groups=SECOND
    )
    got, other, hole = lax.optimization_barrier((got, other, hole))
    swapped = lax.ppermute(got[:, 2 * SLOTS :], "c", [(0, 1), (1, 0)])
    total = call(
        particle_kernel,
        (got, own, other),
        (2, 8, 4, 8, BS),
        "particle",
        in_specs=[VMEM, VMEM, pl.BlockSpec(memory_space=pl.ANY)],
        scratch=[pltpu.VMEM((SLOTS, BS, BS), jnp.float32), pltpu.SemaphoreType.DMA],
    )
    parts = call(terms_kernel, (total, got, swapped, hole), (8, 8, 8, BS), "terms")
    parts = lax.all_to_all(parts, ("c", "x"), 0, 0, tiled=True)
    return call(add_kernel, (parts,), (BS, BS), "add_terms")


def solution(mesh):
    fine = Mesh(mesh.devices.reshape(8, 8, 2, 4), ("z", "y", "c", "x"))
    placed = (P(PLANE, "x"), P("x", PLANE), P(), P("x", None), P())
    return jax.shard_map(
        per_device, mesh=fine, in_specs=placed, out_specs=P("x", PLANE), check_vma=False
    )
```

```python
import jax
import jax.numpy as jnp
from jax import lax
from jax.experimental import pallas as pl
from jax.experimental.pallas import tpu as pltpu
from jax.sharding import Mesh
from jax.sharding import PartitionSpec as P

BS = 128
PLANE = ("z", "y", "c")
SLOTS = 8
MIB = 1024 * 1024
VMEM = pl.BlockSpec(memory_space=pltpu.VMEM)
SMEM = pl.BlockSpec(memory_space=pltpu.SMEM)
HBM = pl.BlockSpec(memory_space=pltpu.HBM)


def pair_of(z, y, c):
    return z * 16 + y * 2 + c


FIRST = [[pair_of(z, y, 0) for z in range(8)] for y in range(8)] + [
    [pair_of(z, y, 1) for y in range(8)] for z in range(8)
]
SECOND = [[pair_of(z, y, 0) for y in range(8)] for z in range(8)] + [
    [pair_of(z, y, 1) for z in range(8)] for y in range(8)
]


def places():
    return tuple(lax.axis_index(a) for a in ("x", "z", "y", "c"))


def call(kernel, args, out, name, in_specs=None, out_specs=VMEM, scratch=(), limit=16):
    return pl.pallas_call(
        kernel,
        in_specs=in_specs or [VMEM] * len(args),
        out_specs=out_specs,
        out_shape=jax.ShapeDtypeStruct(out, jnp.float32),
        scratch_shapes=list(scratch),
        compiler_params=pltpu.CompilerParams(vmem_limit_bytes=limit * MIB),
        name=name,
    )(*args)


def halves(low, high):
    rows = lax.broadcasted_iota(jnp.int32, (8, BS), 0)
    return jnp.where(rows < 4, low, high)


def swap(tile):
    return pltpu.roll(tile, 4, 0)


def spread_kernel(held, out):
    for k in range(8):
        out[k] = held[...]


def spread(held):
    return call(spread_kernel, (held,), (8,) + held.shape, "spread", limit=60)


def pack_kernel(slots, held, out, turned, ready, sems):
    x, z, y, c = places()
    for b in range(32):
        at = slice(b * BS, (b + 1) * BS)
        for t in range(4):
            for h in range(2):
                turned[b, t, 4 * h : 4 * h + 4] = held[2 * t + h, :, at]

    def copy(dest):
        return pltpu.make_async_copy(ready.at[dest], out.at[dest], sems.at[dest])

    def send(dest, _):
        own = jnp.where(c == 0, z * 16 + dest * 2, dest * 16 + y * 2 + 1)
        other = own + 1 - 2 * c
        for side, column in enumerate((own, other)):
            for s in range(SLOTS):
                ready[dest, side * SLOTS + s] = turned[slots[s, column]]
            ready[dest, 2 * SLOTS + side] = turned[column % 32]
        copy(dest).start()
        return 0

    lax.fori_loop(0, 8, send, 0)
    for dest in range(8):
        copy(dest).wait()


def pack(slots, held):
    shape = (8, 2 * SLOTS + 2, 4, 8, BS)
    return call(
        pack_kernel,
        (slots, held),
        shape,
        "pack",
        in_specs=[SMEM, VMEM],
        out_specs=HBM,
        scratch=[
            pltpu.VMEM((32, 4, 8, BS), jnp.float32),
            pltpu.VMEM(shape, jnp.float32),
            pltpu.SemaphoreType.DMA((8,)),
        ],
        limit=52,
    )


def take_kernel(slots, ints, out, sems):
    x, z, y, c = places()
    mine = pair_of(z, y, c)
    copies = []
    for s in range(SLOTS):
        rows = pl.ds(pl.multiple_of(slots[s, mine] * BS, BS), BS)
        copies.append(pltpu.make_async_copy(ints.at[rows], out.at[s], sems.at[s]))
        copies[-1].start()
    for copy in copies:
        copy.wait()


def take(slots, ints):
    return call(
        take_kernel,
        (slots, ints),
        (SLOTS, BS, BS),
        "take",
        in_specs=[SMEM, pl.BlockSpec(memory_space=pl.ANY)],
        scratch=[pltpu.SemaphoreType.DMA((SLOTS,))],
        limit=4,
    )


def parted(value):
    high = value.astype(jnp.bfloat16)
    return high, (value - high.astype(jnp.float32)).astype(jnp.bfloat16)


def product(left, right):
    dot = lambda a, b: jnp.dot(a, b, preferred_element_type=jnp.float32)
    (a, b), (p, q) = parted(left), parted(right)
    wide = dot(a, jnp.concatenate([p, q], axis=1))
    width = right.shape[1]
    return wide[:, :width] + (wide[:, width:] + dot(b, p))


def split_kernel(own, other, rows, own_out, other_out, rows_out):
    rows_out[...] = rows[...]
    for blocks, out in ((own, own_out), (other, other_out)):
        for s in range(0, SLOTS, 2):
            high, low = parted(blocks[s : s + 2].reshape(2 * BS, BS))
            out[s // 2] = jnp.concatenate([high, low], axis=1)


def split(own, other, rows):
    wide = jax.ShapeDtypeStruct((SLOTS // 2, 2 * BS, 2 * BS), jnp.bfloat16)
    return pl.pallas_call(
        split_kernel,
        in_specs=[VMEM] * 3,
        out_specs=[VMEM] * 3,
        out_shape=[wide, wide, jax.ShapeDtypeStruct(rows.shape, rows.dtype)],
        compiler_params=pltpu.CompilerParams(vmem_limit_bytes=16 * MIB),
        name="split",
    )(own, other, rows)


def particle_kernel(got, own, other, out):
    column = lambda at: got[:, at].reshape(256, BS)
    for side, blocks in enumerate((own, other)):
        total = jnp.zeros((512, 2 * BS), jnp.float32)
        for s in range(0, SLOTS, 2):
            at = side * SLOTS + s
            rows = jnp.concatenate([column(at), column(at + 1)], axis=1)
            total += jnp.dot(
                jnp.concatenate(parted(rows), axis=0),
                blocks[s // 2],
                preferred_element_type=jnp.float32,
            )
        low = total[256:, :BS] + (total[:256, BS:] + total[256:, BS:])
        out[side] = (total[:256, :BS] + low).reshape(8, 4, 8, BS)


def terms_kernel(total, got, swapped, hole, out):
    x, z, y, c = places()
    firsts = (c, 1 - c)
    for side in range(2):

        @pl.when(c == 0)
        def _():
            for i in range(4):
                out[firsts[side] + 2 * i] = total[side, :, i]

        @pl.when(c == 1)
        def _():
            for i in range(4):
                out[firsts[side] + 2 * i] = total[side, 2 * i : 2 * i + 2].reshape(8, 8, BS)

        @pl.when(x == z // 2)
        def _():
            rows = jnp.concatenate(
                [
                    got[:, 2 * SLOTS + side].reshape(256, BS),
                    swapped[:, 1 - side].reshape(256, BS),
                ],
                axis=0,
            )
            ladder = product(hole[...].reshape(256, 512), rows).reshape(4, 8, 8, BS)
            for i in range(4):
                out[firsts[side] + 2 * i] += ladder[i]


def add_kernel(parts, out):
    a, b = (parts[k] + parts[k + 2] + parts[k + 4] + parts[k + 6] for k in (0, 1))
    for low in range(2):
        for row in range(8):
            u, v = a[row], b[low * 4 + row // 2]
            at = (low * 8 + row) * 8
            out[at : at + 8] = halves(swap(u) if low else u, v if row % 2 else swap(v))


def slots_of(mask, x):
    slab = lax.dynamic_slice(mask, (x * 32, 0), (32, BS))
    ids = jnp.arange(32, dtype=jnp.int32)
    upto = (ids[:, None] >= ids[None, :]).astype(jnp.float32)
    rank = jnp.dot(upto, slab.astype(jnp.float32)).astype(jnp.int32)
    want = jnp.arange(1, SLOTS + 1, dtype=jnp.int32)
    hit = (rank[None] == want[:, None, None]) & (slab[None] == 1)
    return jnp.sum(jnp.where(hit, ids[None, :, None], 0), axis=1, dtype=jnp.int32)


def per_device(amplitudes, virt_ints, virt_mask, hole_ints, hole_mask):
    x, z, y, c = places()
    held = lax.all_to_all(
        spread(amplitudes),
        PLANE, 0, 0, tiled=True, axis_index_groups=FIRST,
    )
    slots = slots_of(virt_mask, x)
    own = take(slots, virt_ints)
    other = lax.ppermute(own, "c", [(0, 1), (1, 0)])
    held, own = lax.optimization_barrier((held, own))

    keep = jnp.repeat(lax.dynamic_slice(hole_mask, (x, 0), (1, 4)), BS, axis=1).astype(jnp.float32)
    ids = jnp.arange(512, dtype=jnp.int32)
    second, first, r = ids % 256 // 32, ids // 4 % 8, ids % 4
    kind = jnp.where(ids < 256, c, 1 - c)
    wanted = jnp.where(kind == 0, first * 64 + second * 8, second * 64 + first * 8 + 4) + r
    columns = (ids[:, None] == wanted[None, :]).astype(jnp.float32)
    row = jnp.arange(64, dtype=jnp.int32)
    start = jnp.where(c == 0, row // 4 % 2 * 64 + row // 8 * 8, row // 4 * 8 + 4) + row % 4
    rows = (start[:, None] == ids[None, :BS]).astype(jnp.float32)
    exact = lambda a, b: jnp.dot(a, b, precision=lax.Precision.HIGHEST)
    hole_rows = exact(exact(rows, hole_ints * keep), columns)
    own, other, hole_rows = split(own, other, hole_rows)
    hole = lax.all_gather(hole_rows, "x")

    got = lax.all_to_all(
        pack(slots, held), PLANE, 0, 0, tiled=True, axis_index_groups=SECOND
    )
    got, hole = lax.optimization_barrier((got, hole))
    swapped = lax.ppermute(got[:, 2 * SLOTS :], "c", [(0, 1), (1, 0)])
    total = call(particle_kernel, (got, own, other), (2, 8, 4, 8, BS), "particle")
    parts = call(terms_kernel, (total, got, swapped, hole), (8, 8, 8, BS), "terms")
    parts = lax.all_to_all(parts, ("x", "c"), 0, 0, tiled=True)
    return call(add_kernel, (parts,), (BS, BS), "add_terms")


def solution(mesh):
    fine = Mesh(mesh.devices.reshape(8, 8, 2, 4), ("z", "y", "c", "x"))
    placed = (P(PLANE, "x"), P("x", PLANE), P(), P("x", None), P())
    return jax.shard_map(
        per_device, mesh=fine, in_specs=placed, out_specs=P("x", PLANE), check_vma=False
    )
```
